32 devices in a mesh: sa: 4 (over x, core), an: 8 (over z, y).
Axes of the slice: x: 2, y: 2, z: 4, core: 2. Of those that a mesh axis runs over, the one named last changes fastest.
Arguments:
- decoder_states: bfloat16 [4096, 4096], P('sa', 'an'), may hold values from -170 to 170
- w_query: bfloat16 [4096, 4096], P(None, 'an'), may hold values from -0.09375 to 0.09375
- w_key: bfloat16 [1024, 4096], P(None, 'an'), may hold values from -0.1875 to 0.1875
- w_value: bfloat16 [1024, 4096], P(None, 'an'), may hold values from -0.1875 to 0.1875
- w_out: bfloat16 [4096, 4096], P('an'), may hold values from -0.375 to 0.375
- enc_up: bfloat16 [1024, 4096], replicated, may hold values from -0.1875 to 0.1875
- enc_down: bfloat16 [4096, 1024], replicated, may hold values from -0.09375 to 0.09375
- neighbour_inputs: bfloat16 [256, 128, 1024], P(('sa', 'an')), may hold values from -6 to 6
- requests: int32 [128], P('sa'), may hold values from 0 to 63, as said below
Outputs:
- cross_output: bfloat16 [4096, 4096], P('sa', 'an')
The draws below stay inside these ranges and needn't reach their ends.
Inputs may be any that keep to these rules, and one draw needn't show every extreme that they name: Within each block of 32 requests (one index of sa) the owner of a request is its value // 8; no owner receives more than 8 requests of a block and no more than 4 distinct neighbours of one owner are requested in a block; in every block some owner receives exactly 8 requests, 4 of them distinct. A neighbour may be requested several times.
All inputs are finite; a program needn't handle non-finite values.
Results may differ from the reference program's by a relative error of at most 0.01.
The reference program's roundings to bfloat16 on the way (of `chosen`, `normed`, `hidden`, `encoded`, `queries`, `probs` and `attended`) count: a program that leaves them out, or rounds other values in their place, can miss the bound.
Values may be sent and summed in bfloat16 or wider, within the bound.
No kernel may reach another device: no remote copies, remote signals or barrier semaphores. Data moves between devices by JAX's collectives and lax.ppermute only.
A program may use at most 128 MiB of HBM per device.

```python
import jax
import jax.numpy as jnp
import numpy as np
from jax import lax

D = 4096
HEADS = 32
E = 1024
FFE = 4096
GROUP = 64
NT = 128
NEIGH = 2
CH_ROW = 16
NB_OWN = 8
TOKENS = 4096
POOL = 256
N_SA = 4
N_AN = 8


def draw_decoder_states(key, part):
    first = jax.random.fold_in(key, 0)
    base = jax.random.normal(first, (TOKENS, D), jnp.float32)
    return jnp.clip(base, -6.0, 6.0).astype(jnp.bfloat16)


def draw_requests(key, part):
    average = NEIGH * CH_ROW // N_AN
    counts = np.array([2 * average if o % 4 == 0 else average if o % 4 == 1 else average // 2 for o in range(N_AN)])
    distinct = np.maximum(counts // 2, 1)
    slot_table = np.repeat(np.arange(N_AN), counts)
    within = np.concatenate([np.arange(c) for c in counts])
    repeat_of = within % distinct[slot_table]

    def one_row(row_key):
        key_list = jax.random.split(row_key, N_AN + 2)
        owners = jax.random.permutation(key_list[0], N_AN)
        local_ids = jax.vmap(lambda k: jax.random.permutation(k, NB_OWN))(key_list[2:])
        pool_ids = owners[slot_table] * NB_OWN + local_ids[slot_table, repeat_of]
        shuffle = jax.random.permutation(key_list[1], NEIGH * CH_ROW)
        return pool_ids[shuffle]
    all_rows = jax.vmap(one_row)(jax.random.split(jax.random.fold_in(key, 7), N_SA))
    return all_rows.reshape(-1).astype(jnp.int32)


def with_spikes(drawn, key, source, target, shards_of, factor):
    owner, partner = [(jnp.arange(drawn.shape[position]) // (drawn.shape[position] // shards_of)).reshape([-1 if axis == position else 1 for axis in range(drawn.ndim)]) for position in (source, target)]
    chosen = jax.random.permutation(key, shards_of)[partner]
    strong = (owner == chosen) | (owner == (partner + shards_of // 2) % shards_of)
    return jnp.where(strong, factor * drawn, drawn)


def block_scale(stream_key, shape, pieces, least, largest):
    loudness, own = 1.0, jax.random.fold_in(stream_key, 6)
    for dim, blocks in pieces:
        steps = jnp.exp(jax.random.uniform(jax.random.fold_in(own, dim), (blocks,), jnp.float32, least / len(pieces), largest / len(pieces)))
        loudness = loudness * jnp.repeat(steps, shape[dim] // blocks).reshape([-1 if axis == dim else 1 for axis in range(len(shape))])
    return loudness


def bell_draw(own_key, dims, scale, bound, pieces=(), held_as=jnp.bfloat16):
    level = block_scale(own_key, dims, pieces, -0.22, 0.18) if pieces else 1.0
    result = jax.random.normal(own_key, dims, jnp.float32) * scale * level
    return jnp.minimum(jnp.maximum(result, -bound), bound).astype(held_as)


def noise_with(key, dims, spread, reach, cuts, heavy, kind=jnp.bfloat16):
    values = spread * jax.random.normal(key, dims, jnp.float32)
    if cuts:
        values = values * block_scale(key, dims, cuts, -0.22, 0.18)
    return jnp.clip(with_spikes(values, jax.random.fold_in(key, 3), *heavy), -reach, reach).astype(kind)


def setup_inputs(seed: int = 0) -> dict:
    arg_keys = jax.random.split(jax.random.key(seed), 10)
    return {
        "decoder_states": draw_decoder_states(jax.random.fold_in(arg_keys[9], 71), 0),
        "w_query": bell_draw(arg_keys[1], (D, D), D ** -0.5, 0.09375, ((1, 8),)),
        "w_key": bell_draw(arg_keys[2], (E, D), E ** -0.5, 0.1875, ((1, 8),)),
        "w_value": bell_draw(arg_keys[3], (E, D), E ** -0.5, 0.1875, ((1, 8),)),
        "w_out": noise_with(arg_keys[4], (D, D), (D // 8) ** -0.5, 0.375, ((0, 8),), (0, 1, 8, 2.0)),
        "enc_up": bell_draw(arg_keys[5], (E, FFE), E ** -0.5, 0.1875),
        "enc_down": bell_draw(arg_keys[6], (FFE, E), FFE ** -0.5, 0.09375),
        "neighbour_inputs": bell_draw(arg_keys[7], (POOL, NT, E), 1.0, 6.0, ((0, 32),)),
        "requests": draw_requests(jax.random.fold_in(arg_keys[9], 71), 0),
    }


EPS = 1e-06

def encode(rows, enc_up, enc_down):
    wide = rows.astype(jnp.float32)
    square = lax.optimization_barrier(jnp.mean(wide * wide, axis=-1, keepdims=True))
    normed = (wide * lax.rsqrt(square + EPS)).astype(jnp.bfloat16)
    hidden = jax.nn.gelu(jnp.dot(normed, enc_up, preferred_element_type=jnp.float32), approximate=False).astype(jnp.bfloat16)
    return (wide + jnp.dot(hidden, enc_down, preferred_element_type=jnp.float32)).astype(jnp.bfloat16)

def reference(decoder_states, w_query, w_key, w_value, w_out, enc_up, enc_down, neighbour_inputs, requests):
    head_dim = D // HEADS
    scale = float(head_dim) ** (-0.5)
    tok_row = CH_ROW * GROUP
    req_row = NEIGH * CH_ROW
    pool_row = N_AN * NB_OWN

    def one_row(row):
        states = lax.dynamic_slice_in_dim(decoder_states, row * tok_row, tok_row, 0)
        wanted = lax.dynamic_slice_in_dim(requests, row * req_row, req_row, 0)
        pool = lax.dynamic_slice_in_dim(neighbour_inputs, row * pool_row, pool_row, 0)
        chosen = pool[wanted].reshape(req_row * NT, E)
        encoded = encode(chosen, enc_up, enc_down)
        keys = jnp.dot(encoded, w_key, preferred_element_type=jnp.float32).astype(jnp.bfloat16)
        values = jnp.dot(encoded, w_value, preferred_element_type=jnp.float32).astype(jnp.bfloat16)
        keys = keys.reshape(CH_ROW, NEIGH * NT, HEADS, head_dim).astype(jnp.float32)
        values = values.reshape(CH_ROW, NEIGH * NT, HEADS, head_dim).astype(jnp.float32)
        queries = jnp.dot(states, w_query, preferred_element_type=jnp.float32).astype(jnp.bfloat16)
        queries = queries.reshape(CH_ROW, GROUP, HEADS, head_dim).astype(jnp.float32)
        scores = jnp.einsum('cqhd,ckhd->chqk', queries, keys) * scale
        top = lax.optimization_barrier(jnp.max(scores, axis=-1, keepdims=True))
        weights = jnp.exp(scores - top)
        probs = (weights / lax.optimization_barrier(jnp.sum(weights, axis=-1, keepdims=True))).astype(jnp.bfloat16)
        attended = jnp.einsum('chqk,ckhd->cqhd', probs.astype(jnp.float32), values).astype(jnp.bfloat16)
        attended = attended.reshape(tok_row, D)
        return jnp.dot(attended, w_out, preferred_element_type=jnp.float32).astype(jnp.bfloat16)
    outputs = lax.map(one_row, jnp.arange(N_SA, dtype=jnp.int32))
    return outputs.reshape(N_SA * tok_row, D)
```

```python
import functools

import jax
import jax.numpy as jnp
from jax import lax
from jax.experimental import pallas as pl
from jax.experimental.pallas import tpu as pltpu
from jax.sharding import PartitionSpec as P

D = 4096
HEADS = 32
GROUP = 64
NEIGH = 2
EPS = 1e-06
F32 = jnp.float32
BF16 = jnp.bfloat16
VMEM_LIMIT = 56 * 1024 * 1024


def encode_kernel(count, slots, *refs):
    rows = refs[:count]
    up, down, out, wide, normed, total = refs[count:]
    step = pl.program_id(0)
    span = rows[0].shape[1]

    @pl.when(step == 0)
    def _():
        for k in range(count):
            part = pl.ds(k * span, span)
            x = rows[k][0].astype(F32)
            square = jnp.mean(x * x, axis=-1, keepdims=True)
            normed[part, :] = (x * lax.rsqrt(square + EPS)).astype(BF16)
            wide[part, :] = rows[k][0]
        total[...] = jnp.zeros_like(total)

    h = jnp.dot(normed[...], up[...], preferred_element_type=F32)
    h = (0.5 * h * (1.0 + lax.erf(h * (0.5**0.5)))).astype(BF16)
    total[...] += jnp.dot(h, down[...], preferred_element_type=F32)

    @pl.when(step == pl.num_programs(0) - 1)
    def _():
        out[...] = (wide[...].astype(F32) + total[...]).astype(BF16)


def encode(neighbours, slots, up, down):
    count = slots.shape[0]
    _, span, width = neighbours.shape
    hidden = up.shape[1]
    tile = min(512, hidden)
    rows = count * span
    one = [
        pl.BlockSpec((1, span, width), functools.partial(lambda k, i, s: (s[k], 0, 0), k))
        for k in range(count)
    ]
    return pl.pallas_call(
        functools.partial(encode_kernel, count),
        grid_spec=pltpu.PrefetchScalarGridSpec(
            num_scalar_prefetch=1,
            grid=(hidden // tile,),
            in_specs=[
                *one,
                pl.BlockSpec((width, tile), lambda i, s: (0, i)),
                pl.BlockSpec((tile, width), lambda i, s: (i, 0)),
            ],
            out_specs=pl.BlockSpec((rows, width), lambda i, s: (0, 0)),
            scratch_shapes=[
                pltpu.VMEM((rows, width), BF16),
                pltpu.VMEM((rows, width), BF16),
                pltpu.VMEM((rows, width), F32),
            ],
        ),
        out_shape=jax.ShapeDtypeStruct((rows, width), BF16),
        compiler_params=pltpu.CompilerParams(vmem_limit_bytes=VMEM_LIMIT),
        cost_estimate=pl.CostEstimate(
            flops=4 * rows * width * hidden,
            bytes_accessed=4 * width * hidden + 4 * rows * width,
            transcendentals=rows * hidden,
        ),
        name="encode",
    )(slots, *([neighbours] * count), up, down)


def attend_kernel(head_dim, where, *refs):
    blocks = refs[:NEIGH]
    q, wk, wv, out = refs[NEIGH:]
    scale = float(head_dim) ** (-0.5)
    rows = jnp.concatenate([b[0] for b in blocks], axis=0)
    keys = jnp.dot(rows, wk[...], preferred_element_type=F32).astype(BF16)
    values = jnp.dot(rows, wv[...], preferred_element_type=F32).astype(BF16)
    for h in range(q.shape[1] // head_dim):
        cols = slice(h * head_dim, (h + 1) * head_dim)
        scores = (
            lax.dot_general(
                q[:, cols], keys[:, cols], (((1,), (1,)), ((), ())), preferred_element_type=F32
            )
            * scale
        )
        top = jnp.max(scores, axis=-1, keepdims=True)
        weights = jnp.exp(scores - top)
        probs = (weights / jnp.sum(weights, axis=-1, keepdims=True)).astype(BF16)
        out[:, cols] = jnp.dot(probs, values[:, cols], preferred_element_type=F32).astype(BF16)


def attend(where, encoded, queries, wk, wv, head_dim):
    tokens, cols = queries.shape
    groups = tokens // GROUP
    _, span, width = encoded.shape
    one = [
        pl.BlockSpec(
            (1, span, width), functools.partial(lambda k, c, s: (s[c * NEIGH + k], 0, 0), k)
        )
        for k in range(NEIGH)
    ]
    keys = groups * NEIGH * span
    return pl.pallas_call(
        functools.partial(attend_kernel, head_dim),
        grid_spec=pltpu.PrefetchScalarGridSpec(
            num_scalar_prefetch=1,
            grid=(groups,),
            in_specs=[
                *one,
                pl.BlockSpec((GROUP, cols), lambda c, s: (c, 0)),
                pl.BlockSpec((width, cols), lambda c, s: (0, 0)),
                pl.BlockSpec((width, cols), lambda c, s: (0, 0)),
            ],
            out_specs=pl.BlockSpec((GROUP, cols), lambda c, s: (c, 0)),
        ),
        out_shape=jax.ShapeDtypeStruct((tokens, cols), BF16),
        compiler_params=pltpu.CompilerParams(vmem_limit_bytes=VMEM_LIMIT),
        cost_estimate=pl.CostEstimate(
            flops=4 * keys * width * cols + 4 * tokens * NEIGH * span * cols,
            bytes_accessed=2 * keys * width + 4 * width * cols + 4 * tokens * cols,
            transcendentals=tokens * NEIGH * span * (cols // head_dim),
        ),
        name="attend",
    )(where, *([encoded] * NEIGH), queries, wk, wv)


def shards(
    decoder_states, w_query, w_key, w_value, w_out, enc_up, enc_down, neighbour_inputs, requests
):
    n = lax.axis_size("an")
    s_total = lax.axis_size("sa")
    position = lax.axis_index("an")
    length = n // 2
    pair, line = position % 2, position // 2
    first = pair == 0
    tok_rows, local = decoder_states.shape
    half = tok_rows // 2
    head_dim = D // HEADS
    total_requests = requests.shape[0]
    per_owner = total_requests // n
    nb_own, span, width = neighbour_inputs.shape

    def swap_pair(a):
        return lax.ppermute(a, "an", [(i, i ^ 1) for i in range(n)])

    def on_line(a, moves):
        return lax.ppermute(a, "an", [(i * 2 + y, j * 2 + y) for i, j in moves for y in range(2)])

    def line_gather(a):
        if length == 4:
            two = on_line(a, [(i, (i + 2) % 4) for i in range(4)])
            after = on_line(a, [(i + 1, i) for i in range(3)])
            before = on_line(a, [(i, i + 1) for i in range(3)])
            ends = on_line(two, [(2, 3), (1, 0)])
            return [
                a,
                jnp.where(line == 3, ends, after),
                two,
                jnp.where(line == 0, ends, before),
            ]
        out = [a]
        for _ in range(length - 1):
            out.append(on_line(out[-1], [((i + 1) % length, i) for i in range(length)]))
        return out

    def line_sum(part):
        if length == 4:
            one, three = part(1).astype(BF16), part(3).astype(BF16)
            relay = on_line(jnp.where(line == 0, three, one), [(0, 1), (3, 2)])
            after = on_line(one, [(i, i + 1) for i in range(3)])
            before = on_line(three, [(i + 1, i) for i in range(3)])
            mine = part(0)
            two = on_line(
                (part(2) + relay.astype(F32)).astype(BF16), [(i, (i + 2) % 4) for i in range(4)]
            )
            return mine + after.astype(F32) + before.astype(F32) + two.astype(F32)
        total = part(length - 1)
        for d in range(length - 2, -1, -1):
            got = on_line(total.astype(BF16), [(i, (i + 1) % length) for i in range(length)])
            total = got.astype(F32) + part(d)
        return total

    def share(a, axis):
        size = a.shape[axis] // s_total
        piece = lax.dynamic_slice_in_dim(a, lax.axis_index("sa") * size, size, axis)
        pieces = [swap_pair(piece)]
        bit = 1
        while bit < s_total:
            pieces += [
                lax.ppermute(p, "sa", [(i, i ^ bit) for i in range(s_total)]) for p in pieces
            ]
            bit *= 2
        return pieces

    low, high = decoder_states[:half], decoder_states[half:]
    mine = jnp.where(first, low, high)
    other = swap_pair(jnp.where(first, high, low))
    mine_line = line_gather(mine)
    other_line = line_gather(other)

    owner = requests // nb_own
    local_id = requests % nb_own
    owner_range = jnp.arange(n, dtype=jnp.int32)
    local_range = jnp.arange(nb_own, dtype=jnp.int32)
    hits = (owner[:, None, None] == owner_range[None, :, None]) & (
        local_id[:, None, None] == local_range[None, None, :]
    )
    present = jnp.max(hits.astype(jnp.int32), axis=0)
    earlier = (local_range[None, :] < local_range[:, None]).astype(jnp.int32)
    ranked = jnp.sum(present[:, None, :] * earlier[None, :, :], axis=2)
    rank_of_request = jnp.sum(jnp.where(hits, ranked[None], 0), axis=(1, 2))
    is_me = owner_range[:, None] == position
    my_present = jnp.sum(jnp.where(is_me, present, 0), axis=0)
    my_rank = jnp.sum(jnp.where(is_me, ranked, 0), axis=0)
    chosen_mask = (my_present[:, None] == 1) & (
        my_rank[:, None] == jnp.arange(per_owner, dtype=jnp.int32)[None, :]
    )
    local_of_slot = jnp.sum(jnp.where(chosen_mask, local_range[:, None], 0), axis=0)
    distance = (owner // 2 - line + length) % length
    crossed = (owner % 2 != pair).astype(jnp.int32)
    where = (distance * 2 + crossed) * per_owner + rank_of_request
    where = jnp.where(first, where[: total_requests // 2], where[total_requests // 2 :])

    key_pieces, value_pieces = share(w_key, 1), share(w_value, 1)
    query_pieces = share(w_query, 1)
    out_pieces = share(w_out, 0)
    wk = jnp.concatenate([w_key, *key_pieces], axis=1)
    wv = jnp.concatenate([w_value, *value_pieces], axis=1)
    wq = jnp.concatenate([w_query, *query_pieces], axis=1)
    wo = jnp.concatenate([w_out, *out_pieces], axis=0)

    encoded = encode(neighbour_inputs, local_of_slot, enc_up, enc_down)
    blocks = []
    for block in line_gather(encoded):
        blocks += [block, swap_pair(block)]
    everything = jnp.concatenate(blocks, axis=0).reshape(n * per_owner, span, width)

    queries = 0.0
    for d in range(length):
        place = (line + d) % length
        for x, y in ((mine_line[d], pair), (other_line[d], 1 - pair)):
            rows = lax.dynamic_slice_in_dim(wq, (place * 2 + y) * local, local, 0)
            queries = queries + jnp.dot(x, rows, preferred_element_type=F32)
    queries = queries.astype(BF16)

    attended = attend(where, everything, queries, wk, wv, head_dim)

    def part(d):
        place = (line + d) % length
        cols = lax.dynamic_slice_in_dim(wo, place * 2 * local, 2 * local, 1)
        return jnp.dot(attended, cols, preferred_element_type=F32)

    summed = line_sum(part).astype(BF16)
    left, right = summed[:, :local], summed[:, local:]
    keep = jnp.where(first, left, right)
    got = swap_pair(jnp.where(first, right, left))
    return jnp.concatenate([jnp.where(first, keep, got), jnp.where(first, got, keep)], axis=0)


def solution(mesh):
    placed = (
        P("sa", "an"),
        P(None, "an"),
        P(None, "an"),
        P(None, "an"),
        P("an", None),
        P(),
        P(),
        P(("sa", "an"), None, None),
        P("sa"),
    )
    return jax.shard_map(
        shards, mesh=mesh, in_specs=placed, out_specs=P("sa", "an"), check_vma=False
    )
```

```python
import functools

import jax
import jax.numpy as jnp
from jax import lax
from jax.experimental import pallas as pl
from jax.experimental.pallas import tpu as pltpu
from jax.sharding import PartitionSpec as P

D = 4096
HEADS = 32
GROUP = 64
NEIGH = 2
EPS = 1e-06
F32 = jnp.float32
BF16 = jnp.bfloat16
MIB = 1024 * 1024


def encode_kernel(count, slots, *refs):
    rows = refs[:count]
    up, down, out, wide, normed, total = refs[count:]
    step = pl.program_id(0)
    span = rows[0].shape[1]

    @pl.when(step == 0)
    def _():
        for k in range(count):
            part = pl.ds(k * span, span)
            x = rows[k][0].astype(F32)
            square = jnp.mean(x * x, axis=-1, keepdims=True)
            normed[part, :] = (x * lax.rsqrt(square + EPS)).astype(BF16)
            wide[part, :] = rows[k][0]
        total[...] = jnp.zeros_like(total)

    h = jnp.dot(normed[...], up[...], preferred_element_type=F32)
    h = (0.5 * h * (1.0 + lax.erf(h * (0.5**0.5)))).astype(BF16)
    total[...] += jnp.dot(h, down[...], preferred_element_type=F32)

    @pl.when(step == pl.num_programs(0) - 1)
    def _():
        out[...] = (wide[...].astype(F32) + total[...]).astype(BF16)


def encode(neighbours, slots, up, down):
    count = slots.shape[0]
    _, span, width = neighbours.shape
    hidden = up.shape[1]
    tile = min(512, hidden)
    rows = count * span
    one = [
        pl.BlockSpec((1, span, width), functools.partial(lambda k, i, s: (s[k], 0, 0), k))
        for k in range(count)
    ]
    return pl.pallas_call(
        functools.partial(encode_kernel, count),
        grid_spec=pltpu.PrefetchScalarGridSpec(
            num_scalar_prefetch=1,
            grid=(hidden // tile,),
            in_specs=[
                *one,
                pl.BlockSpec((width, tile), lambda i, s: (0, i)),
                pl.BlockSpec((tile, width), lambda i, s: (i, 0)),
            ],
            out_specs=pl.BlockSpec((rows, width), lambda i, s: (0, 0)),
            scratch_shapes=[
                pltpu.VMEM((rows, width), BF16),
                pltpu.VMEM((rows, width), BF16),
                pltpu.VMEM((rows, width), F32),
            ],
        ),
        out_shape=jax.ShapeDtypeStruct((rows, width), BF16),
        compiler_params=pltpu.CompilerParams(vmem_limit_bytes=56 * MIB),
        cost_estimate=pl.CostEstimate(
            flops=4 * rows * width * hidden,
            bytes_accessed=4 * width * hidden + 4 * rows * width,
            transcendentals=rows * hidden,
        ),
        name="encode",
    )(slots, *([neighbours] * count), up, down)


def attend_kernel(head_dim, count, where, *refs):
    blocks = refs[:count]
    q, *weights, out, keys, values, scores, probs = refs[count:]
    scale = float(head_dim) ** (-0.5)
    rows = jnp.concatenate([b[0] for b in blocks], axis=0)
    half = q.shape[1] // 2
    for made, (near, far) in ((keys, weights[:2]), (values, weights[2:])):
        made[:, :half] = jnp.dot(rows, near[...], preferred_element_type=F32).astype(BF16)
        made[:, half:] = jnp.dot(rows, far[...], preferred_element_type=F32).astype(BF16)
    groups, heads = count // NEIGH, q.shape[1] // head_dim
    span = rows.shape[0] // groups
    each = [(g, h) for g in range(groups) for h in range(heads)]

    def places(g, h):
        at = (g * heads + h) * GROUP
        return (
            slice(g * GROUP, (g + 1) * GROUP),
            slice(g * span, (g + 1) * span),
            slice(h * head_dim, (h + 1) * head_dim),
            slice(at, at + GROUP),
        )

    for g, h in each:
        mine, seen, cols, at = places(g, h)
        scores[at, :] = (
            lax.dot_general(
                q[mine, cols],
                keys[seen, cols],
                (((1,), (1,)), ((), ())),
                preferred_element_type=F32,
            )
            * scale
        )
    for g in range(groups):
        at = slice(g * heads * GROUP, (g + 1) * heads * GROUP)
        s = scores[at, :]
        weights = jnp.exp(s - jnp.max(s, axis=-1, keepdims=True))
        probs[at, :] = (weights / jnp.sum(weights, axis=-1, keepdims=True)).astype(BF16)
    for g, h in each:
        mine, seen, cols, at = places(g, h)
        out[mine, cols] = jnp.dot(
            probs[at, :], values[seen, cols], preferred_element_type=F32
        ).astype(BF16)


def attend(where, encoded, queries, w_key, w_value, packed, head_dim, at_once):
    tokens, cols = queries.shape
    groups = tokens // GROUP
    _, span, width = encoded.shape
    count = at_once * NEIGH
    one = [
        pl.BlockSpec((1, span, width), functools.partial(lambda k, c, s: (s[c * count + k], 0, 0), k))
        for k in range(count)
    ]
    keys = groups * NEIGH * span
    return pl.pallas_call(
        functools.partial(attend_kernel, head_dim, count),
        grid_spec=pltpu.PrefetchScalarGridSpec(
            num_scalar_prefetch=1,
            grid=(groups // at_once,),
            in_specs=[
                *one,
                pl.BlockSpec((at_once * GROUP, cols), lambda c, s: (c, 0)),
                pl.BlockSpec((width, cols // 2), lambda c, s: (0, 0)),
                pl.BlockSpec((width, cols // 2), lambda c, s: (D // width, 0)),
                pl.BlockSpec((width, cols // 2), lambda c, s: (0, 0)),
                pl.BlockSpec((width, cols // 2), lambda c, s: (D // width + 1, 0)),
            ],
            out_specs=pl.BlockSpec((at_once * GROUP, cols), lambda c, s: (c, 0)),
            scratch_shapes=[
                pltpu.VMEM((count * span, cols), BF16),
                pltpu.VMEM((count * span, cols), BF16),
                pltpu.VMEM((at_once * GROUP * (cols // head_dim), NEIGH * span), F32),
                pltpu.VMEM((at_once * GROUP * (cols // head_dim), NEIGH * span), BF16),
            ],
        ),
        out_shape=jax.ShapeDtypeStruct((tokens, cols), BF16),
        compiler_params=pltpu.CompilerParams(vmem_limit_bytes=40 * MIB),
        cost_estimate=pl.CostEstimate(
            flops=4 * keys * width * cols + 4 * tokens * NEIGH * span * cols,
            bytes_accessed=2 * keys * width + 4 * width * cols + 4 * tokens * cols,
            transcendentals=tokens * NEIGH * span * (cols // head_dim),
        ),
        name="attend",
    )(where, *([encoded] * count), queries, w_key, packed, w_value, packed)


def terms_kernel(order, a, near, far, hold, *send):
    step = pl.program_id(0)
    half = a.shape[1] // 2
    term = jnp.dot(a[:, :half], near[...], preferred_element_type=F32) + jnp.dot(
        a[:, half:], far[...], preferred_element_type=F32
    )

    @pl.when(step == 0)
    def _():
        hold[...] = term

    for k, out in enumerate(send):

        @pl.when(step == k + 1)
        def _(out=out):
            out[...] = term.astype(BF16)


def terms(order, attended, near, far):
    rows, depth = attended.shape
    count = order.shape[0]
    cols = near.shape[1] // count
    return pl.pallas_call(
        terms_kernel,
        grid_spec=pltpu.PrefetchScalarGridSpec(
            num_scalar_prefetch=1,
            grid=(count,),
            in_specs=[
                pl.BlockSpec((rows, depth), lambda k, s: (0, 0)),
                pl.BlockSpec((depth // 2, cols), lambda k, s: (0, s[k])),
                pl.BlockSpec((depth // 2, cols), lambda k, s: (0, s[k])),
            ],
            out_specs=[pl.BlockSpec((rows, cols), lambda k, s: (0, 0))] * count,
        ),
        out_shape=[
            jax.ShapeDtypeStruct((rows, cols), BF16 if k else F32) for k in range(count)
        ],
        compiler_params=pltpu.CompilerParams(vmem_limit_bytes=28 * MIB),
        cost_estimate=pl.CostEstimate(
            flops=2 * rows * depth * cols * count,
            bytes_accessed=2 * rows * depth + 2 * depth * cols * count + 2 * rows * cols * count,
            transcendentals=0,
        ),
        name="terms",
    )(order, attended, near, far)


def shards(
    decoder_states, w_query, w_key, w_value, w_out, enc_up, enc_down, neighbour_inputs, requests
):
    n = lax.axis_size("an")
    s_total = lax.axis_size("sa")
    position = lax.axis_index("an")
    length = n // 2
    pair, line = position % 2, position // 2
    first = pair == 0
    tok_rows, local = decoder_states.shape
    half = tok_rows // 2
    head_dim = D // HEADS
    total_requests = requests.shape[0]
    per_owner = total_requests // n
    nb_own, span, width = neighbour_inputs.shape

    def swap_pair(a):
        return lax.ppermute(a, "an", [(i, i ^ 1) for i in range(n)])

    def swap_sa(a, bit):
        return lax.ppermute(a, "sa", [(i, i ^ bit) for i in range(s_total)])

    def on_line(a, moves):
        return lax.ppermute(a, "an", [(i * 2 + y, j * 2 + y) for i, j in moves for y in range(2)])

    def from_place(a, d):
        return on_line(a, [((i + d) % length, i) for i in range(length)])

    def line_gather(a):
        if length != 4:
            moves = [from_place(a, d) for d in range(1, length)]
            return moves, lambda moves: [a, *moves]
        two = from_place(a, 2)
        after = on_line(a, [(i + 1, i) for i in range(3)])
        before = on_line(a, [(i, i + 1) for i in range(3)])

        def finish(moves):
            two, after, before = moves
            ends = on_line(two, [(2, 3), (1, 0)])
            after = jnp.where(line == 3, ends, after)
            return [a, after, two, jnp.where(line == 0, ends, before)]

        return [two, after, before], finish

    def line_sum(hold, send):
        if length == 4:
            one, two, three = send
            relay = on_line(jnp.where(line == 0, three, one), [(0, 1), (3, 2)])
            after = on_line(one, [(i, i + 1) for i in range(3)])
            before = on_line(three, [(i + 1, i) for i in range(3)])
            two = from_place((two.astype(F32) + relay.astype(F32)).astype(BF16), 2)
            got = [after, before, two]
        else:
            got = [from_place(a, length - 1 - i) for i, a in enumerate(send)]
        for a in got:
            hold = hold + a.astype(F32)
        return hold

    def swap_pieces(pieces, bit, axis):
        return jnp.concatenate([pieces, swap_sa(pieces, bit)], axis=axis)

    def own_piece(a, axis):
        size = a.shape[axis] // s_total
        return lax.dynamic_slice_in_dim(a, lax.axis_index("sa") * size, size, axis)

    low, high = decoder_states[:half], decoder_states[half:]
    mine = jnp.where(first, low, high)
    other = swap_pair(jnp.where(first, high, low))
    owner = requests // nb_own
    local_id = requests % nb_own
    owner_range = jnp.arange(n, dtype=jnp.int32)
    local_range = jnp.arange(nb_own, dtype=jnp.int32)
    hits = (owner[:, None, None] == owner_range[None, :, None]) & (
        local_id[:, None, None] == local_range[None, None, :]
    )
    present = jnp.max(hits.astype(jnp.int32), axis=0)
    earlier = (local_range[None, :] < local_range[:, None]).astype(jnp.int32)
    ranked = jnp.sum(present[:, None, :] * earlier[None, :, :], axis=2)
    rank_of_request = jnp.sum(jnp.where(hits, ranked[None], 0), axis=(1, 2))
    is_me = owner_range[:, None] == position
    my_present = jnp.sum(jnp.where(is_me, present, 0), axis=0)
    my_rank = jnp.sum(jnp.where(is_me, ranked, 0), axis=0)
    chosen_mask = (my_present[:, None] == 1) & (
        my_rank[:, None] == jnp.arange(per_owner, dtype=jnp.int32)[None, :]
    )
    local_of_slot = jnp.sum(jnp.where(chosen_mask, local_range[:, None], 0), axis=0)
    where = owner * per_owner + rank_of_request
    where = jnp.where(first, where[: total_requests // 2], where[total_requests // 2 :])

    tie = lax.optimization_barrier
    bits = [s_total >> k for k in range(1, s_total.bit_length())]
    packed = swap_pair(
        jnp.concatenate([own_piece(w, 1) for w in (w_query, w_key, w_value)], axis=0)
    )
    mine_near, mine_finish = line_gather(mine)
    encoded = encode(neighbour_inputs, local_of_slot, enc_up, enc_down)
    encoded, mine_near, other, packed, piece = tie(
        (encoded, mine_near, other, packed, own_piece(w_out, 0))
    )
    other_near, other_finish = line_gather(other)
    everything = lax.all_gather(
        encoded.reshape(per_owner, span, width), "an", axis=0, tiled=True
    )
    mine_line, other_line = mine_finish(mine_near), other_finish(other_near)
    piece = swap_pair(piece)
    packed = swap_pieces(packed, bits[0], 1)
    mine_line, other_line, packed, piece = tie((mine_line, other_line, packed, piece))
    for bit in bits[1:]:
        packed = swap_pieces(packed, bit, 1)
    for bit in bits:
        piece = swap_pieces(piece, bit, 0)
    order = (line + jnp.arange(length, dtype=jnp.int32)) % length
    everything, piece = tie((everything, piece))

    chunks = []
    split = 1
    rows, asked = half // split, where.shape[0] // split
    for k in range(split):
        queries = []
        for weight in (w_query, packed[:D]):
            total = 0.0
            for d in range(length):
                for x, y in ((mine_line[d], pair), (other_line[d], 1 - pair)):
                    part = lax.dynamic_slice_in_dim(
                        weight, (order[d] * 2 + y) * local, local, 0
                    )
                    total = total + jnp.dot(x, part, preferred_element_type=F32)
            queries.append(total.astype(BF16))
        queries = jnp.concatenate(queries, axis=1)
        attended = attend(
            where[k * asked : (k + 1) * asked],
            everything,
            queries,
            w_key,
            w_value,
            packed,
            head_dim,
            min(4, asked // NEIGH),
        )
        hold, *send = terms(order, attended, w_out, piece)
        summed = line_sum(hold, send).astype(BF16)
        left, right = summed[:, :local], summed[:, local:]
        chunks.append((jnp.where(first, left, right), swap_pair(jnp.where(first, right, left))))
    keep = jnp.concatenate([c[0] for c in chunks], axis=0)
    got = jnp.concatenate([c[1] for c in chunks], axis=0)
    return jnp.concatenate([jnp.where(first, keep, got), jnp.where(first, got, keep)], axis=0)


def solution(mesh):
    placed = (
        P("sa", "an"),
        P(None, "an"),
        P(None, "an"),
        P(None, "an"),
        P("an", None),
        P(),
        P(),
        P(("sa", "an"), None, None),
        P("sa"),
    )
    return jax.shard_map(
        shards, mesh=mesh, in_specs=placed, out_specs=P("sa", "an"), check_vma=False
    )
```

```python
import functools

import jax
import jax.numpy as jnp
from jax import lax
from jax.experimental import pallas as pl
from jax.experimental.pallas import tpu as pltpu
from jax.sharding import PartitionSpec as P

D = 4096
HEADS = 32
GROUP = 64
NEIGH = 2
EPS = 1e-06
F32 = jnp.float32
BF16 = jnp.bfloat16
MIB = 1024 * 1024


def encode_kernel(count, slots, *refs):
    rows = refs[:count]
    up, down, out, wide, normed, total = refs[count:]
    step = pl.program_id(0)
    span = rows[0].shape[1]

    @pl.when(step == 0)
    def _():
        for k in range(count):
            part = pl.ds(k * span, span)
            x = rows[k][0].astype(F32)
            square = jnp.mean(x * x, axis=-1, keepdims=True)
            normed[part, :] = (x * lax.rsqrt(square + EPS)).astype(BF16)
            wide[part, :] = rows[k][0]
        total[...] = jnp.zeros_like(total)

    h = jnp.dot(normed[...], up[...], preferred_element_type=F32)
    h = (0.5 * h * (1.0 + lax.erf(h * (0.5**0.5)))).astype(BF16)
    total[...] += jnp.dot(h, down[...], preferred_element_type=F32)

    @pl.when(step == pl.num_programs(0) - 1)
    def _():
        out[...] = (wide[...].astype(F32) + total[...]).astype(BF16)


def encode(neighbours, slots, up, down):
    count = slots.shape[0]
    _, span, width = neighbours.shape
    hidden = up.shape[1]
    tile = min(512, hidden)
    rows = count * span
    one = [
        pl.BlockSpec((1, span, width), functools.partial(lambda k, i, s: (s[k], 0, 0), k))
        for k in range(count)
    ]
    return pl.pallas_call(
        functools.partial(encode_kernel, count),
        grid_spec=pltpu.PrefetchScalarGridSpec(
            num_scalar_prefetch=1,
            grid=(hidden // tile,),
            in_specs=[
                *one,
                pl.BlockSpec((width, tile), lambda i, s: (0, i)),
                pl.BlockSpec((tile, width), lambda i, s: (i, 0)),
            ],
            out_specs=pl.BlockSpec((rows, width), lambda i, s: (0, 0)),
            scratch_shapes=[
                pltpu.VMEM((rows, width), BF16),
                pltpu.VMEM((rows, width), BF16),
                pltpu.VMEM((rows, width), F32),
            ],
        ),
        out_shape=jax.ShapeDtypeStruct((rows, width), BF16),
        compiler_params=pltpu.CompilerParams(vmem_limit_bytes=56 * MIB),
        cost_estimate=pl.CostEstimate(
            flops=4 * rows * width * hidden,
            bytes_accessed=4 * width * hidden + 4 * rows * width,
            transcendentals=rows * hidden,
        ),
        name="encode",
    )(slots, *([neighbours] * count), up, down)


def attend_kernel(head_dim, count, where, *refs):
    blocks = refs[:count]
    q, *weights, out, keys, values, scores, probs = refs[count:]
    scale = float(head_dim) ** (-0.5)
    rows = jnp.concatenate([b[0] for b in blocks], axis=0)
    half = q.shape[1] // 2
    for made, (near, far) in ((keys, weights[:2]), (values, weights[2:])):
        made[:, :half] = jnp.dot(rows, near[...], preferred_element_type=F32).astype(BF16)
        made[:, half:] = jnp.dot(rows, far[...], preferred_element_type=F32).astype(BF16)
    groups, heads = count // NEIGH, q.shape[1] // head_dim
    span = rows.shape[0] // groups
    each = [(g, h) for g in range(groups) for h in range(heads)]

    def places(g, h):
        at = (g * heads + h) * GROUP
        return (
            slice(g * GROUP, (g + 1) * GROUP),
            slice(g * span, (g + 1) * span),
            slice(h * head_dim, (h + 1) * head_dim),
            slice(at, at + GROUP),
        )

    for g, h in each:
        mine, seen, cols, at = places(g, h)
        scores[at, :] = (
            lax.dot_general(
                q[mine, cols],
                keys[seen, cols],
                (((1,), (1,)), ((), ())),
                preferred_element_type=F32,
            )
            * scale
        )
    for g in range(groups):
        at = slice(g * heads * GROUP, (g + 1) * heads * GROUP)
        s = scores[at, :]
        weights = jnp.exp(s - jnp.max(s, axis=-1, keepdims=True))
        probs[at, :] = (weights / jnp.sum(weights, axis=-1, keepdims=True)).astype(BF16)
    for g, h in each:
        mine, seen, cols, at = places(g, h)
        out[mine, cols] = jnp.dot(
            probs[at, :], values[seen, cols], preferred_element_type=F32
        ).astype(BF16)


def attend(where, encoded, queries, w_key, w_value, packed, head_dim, at_once):
    tokens, cols = queries.shape
    groups = tokens // GROUP
    _, span, width = encoded.shape
    count = at_once * NEIGH
    one = [
        pl.BlockSpec((1, span, width), functools.partial(lambda k, c, s: (s[c * count + k], 0, 0), k))
        for k in range(count)
    ]
    keys = groups * NEIGH * span
    return pl.pallas_call(
        functools.partial(attend_kernel, head_dim, count),
        grid_spec=pltpu.PrefetchScalarGridSpec(
            num_scalar_prefetch=1,
            grid=(groups // at_once,),
            in_specs=[
                *one,
                pl.BlockSpec((at_once * GROUP, cols), lambda c, s: (c, 0)),
                pl.BlockSpec((width, cols // 2), lambda c, s: (0, 0)),
                pl.BlockSpec((width, cols // 2), lambda c, s: (D // width, 0)),
                pl.BlockSpec((width, cols // 2), lambda c, s: (0, 0)),
                pl.BlockSpec((width, cols // 2), lambda c, s: (D // width + 1, 0)),
            ],
            out_specs=pl.BlockSpec((at_once * GROUP, cols), lambda c, s: (c, 0)),
            scratch_shapes=[
                pltpu.VMEM((count * span, cols), BF16),
                pltpu.VMEM((count * span, cols), BF16),
                pltpu.VMEM((at_once * GROUP * (cols // head_dim), NEIGH * span), F32),
                pltpu.VMEM((at_once * GROUP * (cols // head_dim), NEIGH * span), BF16),
            ],
        ),
        out_shape=jax.ShapeDtypeStruct((tokens, cols), BF16),
        compiler_params=pltpu.CompilerParams(vmem_limit_bytes=40 * MIB),
        cost_estimate=pl.CostEstimate(
            flops=4 * keys * width * cols + 4 * tokens * NEIGH * span * cols,
            bytes_accessed=2 * keys * width + 4 * width * cols + 4 * tokens * cols,
            transcendentals=tokens * NEIGH * span * (cols // head_dim),
        ),
        name="attend",
    )(where, *([encoded] * count), queries, w_key, packed, w_value, packed)


def terms_kernel(order, a, near, far, hold, *send):
    step = pl.program_id(0)
    half = a.shape[1] // 2
    term = jnp.dot(a[:, :half], near[...], preferred_element_type=F32) + jnp.dot(
        a[:, half:], far[...], preferred_element_type=F32
    )

    @pl.when(step == 0)
    def _():
        hold[...] = term

    for k, out in enumerate(send):

        @pl.when(step == k + 1)
        def _(out=out):
            out[...] = term.astype(BF16)


def terms(order, attended, near, far):
    rows, depth = attended.shape
    count = order.shape[0]
    cols = near.shape[1] // count
    return pl.pallas_call(
        terms_kernel,
        grid_spec=pltpu.PrefetchScalarGridSpec(
            num_scalar_prefetch=1,
            grid=(count,),
            in_specs=[
                pl.BlockSpec((rows, depth), lambda k, s: (0, 0)),
                pl.BlockSpec((depth // 2, cols), lambda k, s: (0, s[k])),
                pl.BlockSpec((depth // 2, cols), lambda k, s: (0, s[k])),
            ],
            out_specs=[pl.BlockSpec((rows, cols), lambda k, s: (0, 0))] * count,
        ),
        out_shape=[
            jax.ShapeDtypeStruct((rows, cols), BF16 if k else F32) for k in range(count)
        ],
        compiler_params=pltpu.CompilerParams(vmem_limit_bytes=28 * MIB),
        cost_estimate=pl.CostEstimate(
            flops=2 * rows * depth * cols * count,
            bytes_accessed=2 * rows * depth + 2 * depth * cols * count + 2 * rows * cols * count,
            transcendentals=0,
        ),
        name="terms",
    )(order, attended, near, far)


def shards(
    decoder_states, w_query, w_key, w_value, w_out, enc_up, enc_down, neighbour_inputs, requests
):
    n = lax.axis_size("an")
    s_total = lax.axis_size("sa")
    position = lax.axis_index("an")
    length = n // 2
    pair, line = position % 2, position // 2
    first = pair == 0
    tok_rows, local = decoder_states.shape
    half = tok_rows // 2
    head_dim = D // HEADS
    total_requests = requests.shape[0]
    per_owner = total_requests // n
    nb_own, span, width = neighbour_inputs.shape

    def swap_pair(a):
        return lax.ppermute(a, "an", [(i, i ^ 1) for i in range(n)])

    def swap_sa(a, bit):
        return lax.ppermute(a, "sa", [(i, i ^ bit) for i in range(s_total)])

    def on_line(a, moves):
        return lax.ppermute(a, "an", [(i * 2 + y, j * 2 + y) for i, j in moves for y in range(2)])

    def from_place(a, d):
        return on_line(a, [((i + d) % length, i) for i in range(length)])

    def line_gather(a):
        if length != 4:
            moves = [from_place(a, d) for d in range(1, length)]
            return moves, lambda moves: [a, *moves]
        two = from_place(a, 2)
        after = on_line(a, [(i + 1, i) for i in range(3)])
        before = on_line(a, [(i, i + 1) for i in range(3)])

        def finish(moves):
            two, after, before = moves
            ends = on_line(two, [(2, 3), (1, 0)])
            after = jnp.where(line == 3, ends, after)
            return [a, after, two, jnp.where(line == 0, ends, before)]

        return [two, after, before], finish

    def line_sum(hold, send):
        if length == 4:
            one, two, three = send
            relay = on_line(jnp.where(line == 0, three, one), [(0, 1), (3, 2)])
            after = on_line(one, [(i, i + 1) for i in range(3)])
            before = on_line(three, [(i + 1, i) for i in range(3)])
            two = from_place((two.astype(F32) + relay.astype(F32)).astype(BF16), 2)
            got = [after, before, two]
        else:
            got = [from_place(a, length - 1 - i) for i, a in enumerate(send)]
        for a in got:
            hold = hold + a.astype(F32)
        return hold

    def swap_pieces(pieces, bit, axis):
        return jnp.concatenate([pieces, swap_sa(pieces, bit)], axis=axis)

    def own_piece(a, axis):
        size = a.shape[axis] // s_total
        return lax.dynamic_slice_in_dim(a, lax.axis_index("sa") * size, size, axis)

    low, high = decoder_states[:half], decoder_states[half:]
    mine = jnp.where(first, low, high)
    other = swap_pair(jnp.where(first, high, low))
    owner = requests // nb_own
    local_id = requests % nb_own
    owner_range = jnp.arange(n, dtype=jnp.int32)
    local_range = jnp.arange(nb_own, dtype=jnp.int32)
    hits = (owner[:, None, None] == owner_range[None, :, None]) & (
        local_id[:, None, None] == local_range[None, None, :]
    )
    present = jnp.max(hits.astype(jnp.int32), axis=0)
    earlier = (local_range[None, :] < local_range[:, None]).astype(jnp.int32)
    ranked = jnp.sum(present[:, None, :] * earlier[None, :, :], axis=2)
    rank_of_request = jnp.sum(jnp.where(hits, ranked[None], 0), axis=(1, 2))
    is_me = owner_range[:, None] == position
    my_present = jnp.sum(jnp.where(is_me, present, 0), axis=0)
    my_rank = jnp.sum(jnp.where(is_me, ranked, 0), axis=0)
    chosen_mask = (my_present[:, None] == 1) & (
        my_rank[:, None] == jnp.arange(per_owner, dtype=jnp.int32)[None, :]
    )
    local_of_slot = jnp.sum(jnp.where(chosen_mask, local_range[:, None], 0), axis=0)
    away = (owner // 2 - line + length) % length
    over = (owner % 2 != pair).astype(jnp.int32)
    where = (away * 2 + over) * per_owner + rank_of_request
    where = jnp.where(first, where[: total_requests // 2], where[total_requests // 2 :])

    tie = lax.optimization_barrier
    bits = [s_total >> k for k in range(1, s_total.bit_length())]
    rows_each = per_owner * span
    everything = jnp.zeros((n * rows_each, width), BF16)

    def put(everything, a, d, over):
        return lax.dynamic_update_slice_in_dim(everything, a, (d * 2 + over) * rows_each, 0)

    mine_near, mine_finish = line_gather(mine)
    encoded = encode(neighbour_inputs, local_of_slot, enc_up, enc_down)
    encoded, other, mine_near = tie((encoded, other, mine_near))

    packed = swap_pair(
        jnp.concatenate([own_piece(w, 1) for w in (w_query, w_key, w_value)], axis=0)
    )
    near, finish = line_gather(encoded)
    crossed = {0: swap_pair(encoded)}
    mine_line = mine_finish(mine_near)
    near, crossed[0], mine_line, packed, piece, encoded, other = tie(
        (near, crossed[0], mine_line, packed, own_piece(w_out, 0), encoded, other)
    )

    blocks = finish(near)
    crossed[length // 2] = swap_pair(blocks[length // 2])
    other_near, other_finish = line_gather(other)
    packed = swap_pieces(packed, bits[0], 1)
    piece = swap_pair(piece)
    blocks, crossed = tie((blocks, crossed))
    for d in range(length):
        everything = put(everything, blocks[d], d, 0)
    for d in crossed:
        everything = put(everything, crossed[d], d, 1)
    late = [swap_pair(blocks[d]) for d in range(length) if d not in crossed]
    other_near, piece, packed = tie((other_near, piece, packed))

    other_line = other_finish(other_near)
    for bit in bits[1:]:
        packed = swap_pieces(packed, bit, 1)
    for bit in bits:
        piece = swap_pieces(piece, bit, 0)
    late, everything = tie((late, everything))
    for d, a in zip([d for d in range(length) if d not in crossed], late):
        everything = put(everything, a, d, 1)
    everything = everything.reshape(n * per_owner, span, width)
    order = (line + jnp.arange(length, dtype=jnp.int32)) % length

    chunks = []
    split = 1
    rows, asked = half // split, where.shape[0] // split
    for k in range(split):
        queries = []
        for weight in (w_query, packed[:D]):
            total = 0.0
            for d in range(length):
                for x, y in ((mine_line[d], pair), (other_line[d], 1 - pair)):
                    part = lax.dynamic_slice_in_dim(
                        weight, (order[d] * 2 + y) * local, local, 0
                    )
                    total = total + jnp.dot(x, part, preferred_element_type=F32)
            queries.append(total.astype(BF16))
        queries = jnp.concatenate(queries, axis=1)
        attended = attend(
            where[k * asked : (k + 1) * asked],
            everything,
            queries,
            w_key,
            w_value,
            packed,
            head_dim,
            min(4, asked // NEIGH),
        )
        hold, *send = terms(order, attended, w_out, piece)
        summed = line_sum(hold, send).astype(BF16)
        left, right = summed[:, :local], summed[:, local:]
        chunks.append((jnp.where(first, left, right), swap_pair(jnp.where(first, right, left))))
    keep = jnp.concatenate([c[0] for c in chunks], axis=0)
    got = jnp.concatenate([c[1] for c in chunks], axis=0)
    return jnp.concatenate([jnp.where(first, keep, got), jnp.where(first, got, keep)], axis=0)


def solution(mesh):
    placed = (
        P("sa", "an"),
        P(None, "an"),
        P(None, "an"),
        P(None, "an"),
        P("an", None),
        P(),
        P(),
        P(("sa", "an"), None, None),
        P("sa"),
    )
    return jax.shard_map(
        shards, mesh=mesh, in_specs=placed, out_specs=P("sa", "an"), check_vma=False
    )
```

```python
import functools

import jax
import jax.numpy as jnp
from jax import lax
from jax.experimental import pallas as pl
from jax.experimental.pallas import tpu as pltpu
from jax.sharding import PartitionSpec as P

D = 4096
HEADS = 32
GROUP = 64
NEIGH = 2
EPS = 1e-06
F32 = jnp.float32
BF16 = jnp.bfloat16
MIB = 1024 * 1024


def encode_kernel(count, slots, *refs):
    rows = refs[:count]
    up, down, out, wide, normed, total = refs[count:]
    step = pl.program_id(0)
    span = rows[0].shape[1]

    @pl.when(step == 0)
    def _():
        for k in range(count):
            part = pl.ds(k * span, span)
            x = rows[k][0].astype(F32)
            square = jnp.mean(x * x, axis=-1, keepdims=True)
            normed[part, :] = (x * lax.rsqrt(square + EPS)).astype(BF16)
            wide[part, :] = rows[k][0]
        total[...] = jnp.zeros_like(total)

    h = jnp.dot(normed[...], up[...], preferred_element_type=F32)
    h = (0.5 * h * (1.0 + lax.erf(h * (0.5**0.5)))).astype(BF16)
    total[...] += jnp.dot(h, down[...], preferred_element_type=F32)

    @pl.when(step == pl.num_programs(0) - 1)
    def _():
        out[...] = (wide[...].astype(F32) + total[...]).astype(BF16)


def encode(neighbours, slots, up, down):
    count = slots.shape[0]
    _, span, width = neighbours.shape
    hidden = up.shape[1]
    tile = min(512, hidden)
    rows = count * span
    one = [
        pl.BlockSpec((1, span, width), functools.partial(lambda k, i, s: (s[k], 0, 0), k))
        for k in range(count)
    ]
    return pl.pallas_call(
        functools.partial(encode_kernel, count),
        grid_spec=pltpu.PrefetchScalarGridSpec(
            num_scalar_prefetch=1,
            grid=(hidden // tile,),
            in_specs=[
                *one,
                pl.BlockSpec((width, tile), lambda i, s: (0, i)),
                pl.BlockSpec((tile, width), lambda i, s: (i, 0)),
            ],
            out_specs=pl.BlockSpec((rows, width), lambda i, s: (0, 0)),
            scratch_shapes=[
                pltpu.VMEM((rows, width), BF16),
                pltpu.VMEM((rows, width), BF16),
                pltpu.VMEM((rows, width), F32),
            ],
        ),
        out_shape=jax.ShapeDtypeStruct((rows, width), BF16),
        compiler_params=pltpu.CompilerParams(vmem_limit_bytes=56 * MIB),
        cost_estimate=pl.CostEstimate(
            flops=4 * rows * width * hidden,
            bytes_accessed=4 * width * hidden + 4 * rows * width,
            transcendentals=rows * hidden,
        ),
        name="encode",
    )(slots, *([neighbours] * count), up, down)


def attend_kernel(head_dim, count, where, *refs):
    blocks = refs[:count]
    q, *weights, out, keys, values, scores, probs = refs[count:]
    scale = float(head_dim) ** (-0.5)
    rows = jnp.concatenate([b[0] for b in blocks], axis=0)
    half = q.shape[1] // 2
    for made, (near, far) in ((keys, weights[:2]), (values, weights[2:])):
        made[:, :half] = jnp.dot(rows, near[...], preferred_element_type=F32).astype(BF16)
        made[:, half:] = jnp.dot(rows, far[...], preferred_element_type=F32).astype(BF16)
    groups, heads = count // NEIGH, q.shape[1] // head_dim
    span = rows.shape[0] // groups
    each = [(g, h) for g in range(groups) for h in range(heads)]

    def places(g, h):
        at = (g * heads + h) * GROUP
        return (
            slice(g * GROUP, (g + 1) * GROUP),
            slice(g * span, (g + 1) * span),
            slice(h * head_dim, (h + 1) * head_dim),
            slice(at, at + GROUP),
        )

    for g, h in each:
        mine, seen, cols, at = places(g, h)
        scores[at, :] = (
            lax.dot_general(
                q[mine, cols],
                keys[seen, cols],
                (((1,), (1,)), ((), ())),
                preferred_element_type=F32,
            )
            * scale
        )
    for g in range(groups):
        at = slice(g * heads * GROUP, (g + 1) * heads * GROUP)
        s = scores[at, :]
        weights = jnp.exp(s - jnp.max(s, axis=-1, keepdims=True))
        probs[at, :] = (weights / jnp.sum(weights, axis=-1, keepdims=True)).astype(BF16)
    for g, h in each:
        mine, seen, cols, at = places(g, h)
        out[mine, cols] = jnp.dot(
            probs[at, :], values[seen, cols], preferred_element_type=F32
        ).astype(BF16)


def attend(where, encoded, queries, w_key, w_value, packed, head_dim, at_once):
    tokens, cols = queries.shape
    groups = tokens // GROUP
    _, span, width = encoded.shape
    count = at_once * NEIGH
    one = [
        pl.BlockSpec((1, span, width), functools.partial(lambda k, c, s: (s[c * count + k], 0, 0), k))
        for k in range(count)
    ]
    keys = groups * NEIGH * span
    return pl.pallas_call(
        functools.partial(attend_kernel, head_dim, count),
        grid_spec=pltpu.PrefetchScalarGridSpec(
            num_scalar_prefetch=1,
            grid=(groups // at_once,),
            in_specs=[
                *one,
                pl.BlockSpec((at_once * GROUP, cols), lambda c, s: (c, 0)),
                pl.BlockSpec((width, cols // 2), lambda c, s: (0, 0)),
                pl.BlockSpec((width, cols // 2), lambda c, s: (D // width, 0)),
                pl.BlockSpec((width, cols // 2), lambda c, s: (0, 0)),
                pl.BlockSpec((width, cols // 2), lambda c, s: (D // width + 1, 0)),
            ],
            out_specs=pl.BlockSpec((at_once * GROUP, cols), lambda c, s: (c, 0)),
            scratch_shapes=[
                pltpu.VMEM((count * span, cols), BF16),
                pltpu.VMEM((count * span, cols), BF16),
                pltpu.VMEM((at_once * GROUP * (cols // head_dim), NEIGH * span), F32),
                pltpu.VMEM((at_once * GROUP * (cols // head_dim), NEIGH * span), BF16),
            ],
        ),
        out_shape=jax.ShapeDtypeStruct((tokens, cols), BF16),
        compiler_params=pltpu.CompilerParams(vmem_limit_bytes=40 * MIB),
        cost_estimate=pl.CostEstimate(
            flops=4 * keys * width * cols + 4 * tokens * NEIGH * span * cols,
            bytes_accessed=2 * keys * width + 4 * width * cols + 4 * tokens * cols,
            transcendentals=tokens * NEIGH * span * (cols // head_dim),
        ),
        name="attend",
    )(where, *([encoded] * count), queries, w_key, packed, w_value, packed)


def terms_kernel(order, a, near, far, hold, *send):
    step = pl.program_id(0)
    half = a.shape[1] // 2
    term = jnp.dot(a[:, :half], near[...], preferred_element_type=F32) + jnp.dot(
        a[:, half:], far[...], preferred_element_type=F32
    )

    @pl.when(step == 0)
    def _():
        hold[...] = term

    for k, out in enumerate(send):

        @pl.when(step == k + 1)
        def _(out=out):
            out[...] = term.astype(BF16)


def terms(order, attended, near, far):
    rows, depth = attended.shape
    count = order.shape[0]
    cols = near.shape[1] // count
    return pl.pallas_call(
        terms_kernel,
        grid_spec=pltpu.PrefetchScalarGridSpec(
            num_scalar_prefetch=1,
            grid=(count,),
            in_specs=[
                pl.BlockSpec((rows, depth), lambda k, s: (0, 0)),
                pl.BlockSpec((depth // 2, cols), lambda k, s: (0, s[k])),
                pl.BlockSpec((depth // 2, cols), lambda k, s: (0, s[k])),
            ],
            out_specs=[pl.BlockSpec((rows, cols), lambda k, s: (0, 0))] * count,
        ),
        out_shape=[
            jax.ShapeDtypeStruct((rows, cols), BF16 if k else F32) for k in range(count)
        ],
        compiler_params=pltpu.CompilerParams(vmem_limit_bytes=28 * MIB),
        cost_estimate=pl.CostEstimate(
            flops=2 * rows * depth * cols * count,
            bytes_accessed=2 * rows * depth + 2 * depth * cols * count + 2 * rows * cols * count,
            transcendentals=0,
        ),
        name="terms",
    )(order, attended, near, far)


def shards(
    decoder_states, w_query, w_key, w_value, w_out, enc_up, enc_down, neighbour_inputs, requests
):
    n = lax.axis_size("an")
    s_total = lax.axis_size("sa")
    position = lax.axis_index("an")
    length = n // 2
    pair, line = position % 2, position // 2
    first = pair == 0
    tok_rows, local = decoder_states.shape
    half = tok_rows // 2
    head_dim = D // HEADS
    total_requests = requests.shape[0]
    per_owner = total_requests // n
    nb_own, span, width = neighbour_inputs.shape

    def swap_pair(a):
        return lax.ppermute(a, "an", [(i, i ^ 1) for i in range(n)])

    def swap_sa(a, bit):
        return lax.ppermute(a, "sa", [(i, i ^ bit) for i in range(s_total)])

    def on_line(a, moves):
        return lax.ppermute(a, "an", [(i * 2 + y, j * 2 + y) for i, j in moves for y in range(2)])

    def from_place(a, d):
        return on_line(a, [((i + d) % length, i) for i in range(length)])

    def line_gather(a):
        if length != 4:
            moves = [from_place(a, d) for d in range(1, length)]
            return moves, lambda moves: [a, *moves]
        two = from_place(a, 2)
        after = on_line(a, [(i + 1, i) for i in range(3)])
        before = on_line(a, [(i, i + 1) for i in range(3)])

        def finish(moves):
            two, after, before = moves
            ends = on_line(two, [(2, 3), (1, 0)])
            after = jnp.where(line == 3, ends, after)
            return [a, after, two, jnp.where(line == 0, ends, before)]

        return [two, after, before], finish

    def sides(a):
        left, right = a[:, :local], a[:, local:]
        return jnp.where(first, left, right), jnp.where(first, right, left)

    def line_sum(hold, send):
        if length == 4:
            one, two, three = send
            relay = on_line(jnp.where(line == 0, three, one), [(0, 1), (3, 2)])
            after = on_line(one, [(i, i + 1) for i in range(3)])
            before = on_line(three, [(i + 1, i) for i in range(3)])
            mine, given = sides((two.astype(F32) + relay.astype(F32)).astype(BF16))
            mine = from_place(mine, 2)
            given = lax.ppermute(given, "an", [(i, (i + 4) % 8 ^ 1) for i in range(n)])
            keep, give = sides(hold + after.astype(F32) + before.astype(F32))
            got = swap_pair(give.astype(BF16))
            return keep + mine.astype(F32), got.astype(F32) + given.astype(F32)
        for i, a in enumerate(send):
            hold = hold + from_place(a, length - 1 - i).astype(F32)
        keep, give = sides(hold)
        return keep, swap_pair(give.astype(BF16))

    def swap_pieces(pieces, bit, axis):
        return jnp.concatenate([pieces, swap_sa(pieces, bit)], axis=axis)

    def own_piece(a, axis):
        size = a.shape[axis] // s_total
        return lax.dynamic_slice_in_dim(a, lax.axis_index("sa") * size, size, axis)

    low, high = decoder_states[:half], decoder_states[half:]
    mine = jnp.where(first, low, high)
    other = swap_pair(jnp.where(first, high, low))
    owner = requests // nb_own
    local_id = requests % nb_own
    owner_range = jnp.arange(n, dtype=jnp.int32)
    local_range = jnp.arange(nb_own, dtype=jnp.int32)
    hits = (owner[:, None, None] == owner_range[None, :, None]) & (
        local_id[:, None, None] == local_range[None, None, :]
    )
    present = jnp.max(hits.astype(jnp.int32), axis=0)
    earlier = (local_range[None, :] < local_range[:, None]).astype(jnp.int32)
    ranked = jnp.sum(present[:, None, :] * earlier[None, :, :], axis=2)
    rank_of_request = jnp.sum(jnp.where(hits, ranked[None], 0), axis=(1, 2))
    is_me = owner_range[:, None] == position
    my_present = jnp.sum(jnp.where(is_me, present, 0), axis=0)
    my_rank = jnp.sum(jnp.where(is_me, ranked, 0), axis=0)
    chosen_mask = (my_present[:, None] == 1) & (
        my_rank[:, None] == jnp.arange(per_owner, dtype=jnp.int32)[None, :]
    )
    local_of_slot = jnp.sum(jnp.where(chosen_mask, local_range[:, None], 0), axis=0)
    away = (owner // 2 - line + length) % length
    over = (owner % 2 != pair).astype(jnp.int32)
    where = (away * 2 + over) * per_owner + rank_of_request
    where = jnp.where(first, where[: total_requests // 2], where[total_requests // 2 :])

    tie = lax.optimization_barrier
    bits = [s_total >> k for k in range(1, s_total.bit_length())]
    rows_each = per_owner * span
    everything = jnp.zeros((n * rows_each, width), BF16)

    def put(everything, a, d, over):
        return lax.dynamic_update_slice_in_dim(everything, a, (d * 2 + over) * rows_each, 0)

    mine_near, mine_finish = line_gather(mine)
    encoded = encode(neighbour_inputs, local_of_slot, enc_up, enc_down)
    encoded, other, mine_near = tie((encoded, other, mine_near))

    packed = swap_pair(
        jnp.concatenate([own_piece(w, 1) for w in (w_query, w_key, w_value)], axis=0)
    )
    near, finish = line_gather(encoded)
    crossed = {0: swap_pair(encoded)}
    mine_line = mine_finish(mine_near)
    near, crossed[0], mine_line, packed, piece, encoded, other = tie(
        (near, crossed[0], mine_line, packed, own_piece(w_out, 0), encoded, other)
    )

    blocks = finish(near)
    crossed[length // 2] = swap_pair(blocks[length // 2])
    other_near, other_finish = line_gather(other)
    packed = swap_pieces(packed, bits[0], 1)
    piece = swap_pair(piece)
    blocks, crossed = tie((blocks, crossed))
    for d in range(length):
        everything = put(everything, blocks[d], d, 0)
    for d in crossed:
        everything = put(everything, crossed[d], d, 1)
    late = [swap_pair(blocks[d]) for d in range(length) if d not in crossed]
    other_near, piece, packed = tie((other_near, piece, packed))

    other_line = other_finish(other_near)
    for bit in bits[1:]:
        packed = swap_pieces(packed, bit, 1)
    for bit in bits:
        piece = swap_pieces(piece, bit, 0)
    late, everything = tie((late, everything))
    for d, a in zip([d for d in range(length) if d not in crossed], late):
        everything = put(everything, a, d, 1)
    everything = everything.reshape(n * per_owner, span, width)
    order = (line + jnp.arange(length, dtype=jnp.int32)) % length

    chunks = []
    split = 1
    rows, asked = half // split, where.shape[0] // split
    for k in range(split):
        queries = []
        for weight in (w_query, packed[:D]):
            total = 0.0
            for d in range(length):
                for x, y in ((mine_line[d], pair), (other_line[d], 1 - pair)):
                    part = lax.dynamic_slice_in_dim(
                        weight, (order[d] * 2 + y) * local, local, 0
                    )
                    total = total + jnp.dot(x, part, preferred_element_type=F32)
            queries.append(total.astype(BF16))
        queries = jnp.concatenate(queries, axis=1)
        attended = attend(
            where[k * asked : (k + 1) * asked],
            everything,
            queries,
            w_key,
            w_value,
            packed,
            head_dim,
            min(4, asked // NEIGH),
        )
        hold, *send = terms(order, attended, w_out, piece)
        chunks.append([a.astype(BF16) for a in line_sum(hold, send)])
    keep = jnp.concatenate([c[0] for c in chunks], axis=0)
    got = jnp.concatenate([c[1] for c in chunks], axis=0)
    return jnp.concatenate([jnp.where(first, keep, got), jnp.where(first, got, keep)], axis=0)


def solution(mesh):
    placed = (
        P("sa", "an"),
        P(None, "an"),
        P(None, "an"),
        P(None, "an"),
        P("an", None),
        P(),
        P(),
        P(("sa", "an"), None, None),
        P("sa"),
    )
    return jax.shard_map(
        shards, mesh=mesh, in_specs=placed, out_specs=P("sa", "an"), check_vma=False
    )
```

```python
import functools

import jax
import jax.numpy as jnp
from jax import lax
from jax.experimental import pallas as pl
from jax.experimental.pallas import tpu as pltpu
from jax.sharding import PartitionSpec as P

D = 4096
HEADS = 32
GROUP = 64
NEIGH = 2
EPS = 1e-06
F32 = jnp.float32
BF16 = jnp.bfloat16
MIB = 1024 * 1024


def encode_kernel(count, slots, *refs):
    rows = refs[:count]
    up, down, out, wide, normed, total = refs[count:]
    step = pl.program_id(0)
    span = rows[0].shape[1]

    @pl.when(step == 0)
    def _():
        for k in range(count):
            part = pl.ds(k * span, span)
            x = rows[k][0].astype(F32)
            square = jnp.mean(x * x, axis=-1, keepdims=True)
            normed[part, :] = (x * lax.rsqrt(square + EPS)).astype(BF16)
            wide[part, :] = rows[k][0]
        total[...] = jnp.zeros_like(total)

    h = jnp.dot(normed[...], up[...], preferred_element_type=F32)
    h = (0.5 * h * (1.0 + lax.erf(h * (0.5**0.5)))).astype(BF16)
    total[...] += jnp.dot(h, down[...], preferred_element_type=F32)

    @pl.when(step == pl.num_programs(0) - 1)
    def _():
        out[...] = (wide[...].astype(F32) + total[...]).astype(BF16)


def encode(neighbours, slots, up, down):
    count = slots.shape[0]
    _, span, width = neighbours.shape
    hidden = up.shape[1]
    tile = min(512, hidden)
    rows = count * span
    one = [
        pl.BlockSpec((1, span, width), functools.partial(lambda k, i, s: (s[k], 0, 0), k))
        for k in range(count)
    ]
    return pl.pallas_call(
        functools.partial(encode_kernel, count),
        grid_spec=pltpu.PrefetchScalarGridSpec(
            num_scalar_prefetch=1,
            grid=(hidden // tile,),
            in_specs=[
                *one,
                pl.BlockSpec((width, tile), lambda i, s: (0, i)),
                pl.BlockSpec((tile, width), lambda i, s: (i, 0)),
            ],
            out_specs=pl.BlockSpec((rows, width), lambda i, s: (0, 0)),
            scratch_shapes=[
                pltpu.VMEM((rows, width), BF16),
                pltpu.VMEM((rows, width), BF16),
                pltpu.VMEM((rows, width), F32),
            ],
        ),
        out_shape=jax.ShapeDtypeStruct((rows, width), BF16),
        compiler_params=pltpu.CompilerParams(vmem_limit_bytes=56 * MIB),
        cost_estimate=pl.CostEstimate(
            flops=4 * rows * width * hidden,
            bytes_accessed=4 * width * hidden + 4 * rows * width,
            transcendentals=rows * hidden,
        ),
        name="encode",
    )(slots, *([neighbours] * count), up, down)


def attend_kernel(head_dim, count, where, *refs):
    blocks = refs[:count]
    q, *weights, out, keys, values, scores, probs = refs[count:]
    scale = float(head_dim) ** (-0.5)
    rows = jnp.concatenate([b[0] for b in blocks], axis=0)
    half = q.shape[1] // 2
    for made, (near, far) in ((keys, weights[:2]), (values, weights[2:])):
        made[:, :half] = jnp.dot(rows, near[...], preferred_element_type=F32).astype(BF16)
        made[:, half:] = jnp.dot(rows, far[...], preferred_element_type=F32).astype(BF16)
    groups, heads = count // NEIGH, q.shape[1] // head_dim
    span = rows.shape[0] // groups
    each = [(g, h) for g in range(groups) for h in range(heads)]

    def places(g, h):
        at = (g * heads + h) * GROUP
        return (
            slice(g * GROUP, (g + 1) * GROUP),
            slice(g * span, (g + 1) * span),
            slice(h * head_dim, (h + 1) * head_dim),
            slice(at, at + GROUP),
        )

    for g, h in each:
        mine, seen, cols, at = places(g, h)
        scores[at, :] = (
            lax.dot_general(
                q[mine, cols],
                keys[seen, cols],
                (((1,), (1,)), ((), ())),
                preferred_element_type=F32,
            )
            * scale
        )
    for g in range(groups):
        at = slice(g * heads * GROUP, (g + 1) * heads * GROUP)
        s = scores[at, :]
        weights = jnp.exp(s - jnp.max(s, axis=-1, keepdims=True))
        probs[at, :] = (weights / jnp.sum(weights, axis=-1, keepdims=True)).astype(BF16)
    for g, h in each:
        mine, seen, cols, at = places(g, h)
        out[mine, cols] = jnp.dot(
            probs[at, :], values[seen, cols], preferred_element_type=F32
        ).astype(BF16)


def attend(where, encoded, queries, w_key, w_value, packed, head_dim, at_once):
    tokens, cols = queries.shape
    groups = tokens // GROUP
    _, span, width = encoded.shape
    count = at_once * NEIGH
    one = [
        pl.BlockSpec((1, span, width), functools.partial(lambda k, c, s: (s[c * count + k], 0, 0), k))
        for k in range(count)
    ]
    keys = groups * NEIGH * span
    return pl.pallas_call(
        functools.partial(attend_kernel, head_dim, count),
        grid_spec=pltpu.PrefetchScalarGridSpec(
            num_scalar_prefetch=1,
            grid=(groups // at_once,),
            in_specs=[
                *one,
                pl.BlockSpec((at_once * GROUP, cols), lambda c, s: (c, 0)),
                pl.BlockSpec((width, cols // 2), lambda c, s: (0, 0)),
                pl.BlockSpec((width, cols // 2), lambda c, s: (D // width, 0)),
                pl.BlockSpec((width, cols // 2), lambda c, s: (0, 0)),
                pl.BlockSpec((width, cols // 2), lambda c, s: (D // width + 1, 0)),
            ],
            out_specs=pl.BlockSpec((at_once * GROUP, cols), lambda c, s: (c, 0)),
            scratch_shapes=[
                pltpu.VMEM((count * span, cols), BF16),
                pltpu.VMEM((count * span, cols), BF16),
                pltpu.VMEM((at_once * GROUP * (cols // head_dim), NEIGH * span), F32),
                pltpu.VMEM((at_once * GROUP * (cols // head_dim), NEIGH * span), BF16),
            ],
        ),
        out_shape=jax.ShapeDtypeStruct((tokens, cols), BF16),
        compiler_params=pltpu.CompilerParams(vmem_limit_bytes=40 * MIB),
        cost_estimate=pl.CostEstimate(
            flops=4 * keys * width * cols + 4 * tokens * NEIGH * span * cols,
            bytes_accessed=2 * keys * width + 4 * width * cols + 4 * tokens * cols,
            transcendentals=tokens * NEIGH * span * (cols // head_dim),
        ),
        name="attend",
    )(where, *([encoded] * count), queries, w_key, packed, w_value, packed)


def terms_kernel(order, a, near, far, hold, *send):
    step = pl.program_id(0)
    half = a.shape[1] // 2
    term = jnp.dot(a[:, :half], near[...], preferred_element_type=F32) + jnp.dot(
        a[:, half:], far[...], preferred_element_type=F32
    )

    @pl.when(step == 0)
    def _():
        hold[...] = term

    for k, out in enumerate(send):

        @pl.when(step == k + 1)
        def _(out=out):
            out[...] = term.astype(BF16)


def terms(order, attended, near, far):
    rows, depth = attended.shape
    count = order.shape[0]
    cols = near.shape[1] // count
    return pl.pallas_call(
        terms_kernel,
        grid_spec=pltpu.PrefetchScalarGridSpec(
            num_scalar_prefetch=1,
            grid=(count,),
            in_specs=[
                pl.BlockSpec((rows, depth), lambda k, s: (0, 0)),
                pl.BlockSpec((depth // 2, cols), lambda k, s: (0, s[k])),
                pl.BlockSpec((depth // 2, cols), lambda k, s: (0, s[k])),
            ],
            out_specs=[pl.BlockSpec((rows, cols), lambda k, s: (0, 0))] * count,
        ),
        out_shape=[
            jax.ShapeDtypeStruct((rows, cols), BF16 if k else F32) for k in range(count)
        ],
        compiler_params=pltpu.CompilerParams(vmem_limit_bytes=28 * MIB),
        cost_estimate=pl.CostEstimate(
            flops=2 * rows * depth * cols * count,
            bytes_accessed=2 * rows * depth + 2 * depth * cols * count + 2 * rows * cols * count,
            transcendentals=0,
        ),
        name="terms",
    )(order, attended, near, far)


def shards(
    decoder_states, w_query, w_key, w_value, w_out, enc_up, enc_down, neighbour_inputs, requests
):
    n = lax.axis_size("an")
    s_total = lax.axis_size("sa")
    position = lax.axis_index("an")
    length = n // 2
    pair, line = position % 2, position // 2
    first = pair == 0
    tok_rows, local = decoder_states.shape
    half = tok_rows // 2
    head_dim = D // HEADS
    total_requests = requests.shape[0]
    per_owner = total_requests // n
    nb_own, span, width = neighbour_inputs.shape

    def swap_pair(a):
        return lax.ppermute(a, "an", [(i, i ^ 1) for i in range(n)])

    def swap_sa(a, bit):
        return lax.ppermute(a, "sa", [(i, i ^ bit) for i in range(s_total)])

    def on_line(a, moves):
        return lax.ppermute(a, "an", [(i * 2 + y, j * 2 + y) for i, j in moves for y in range(2)])

    def from_place(a, d):
        return on_line(a, [((i + d) % length, i) for i in range(length)])

    def line_gather(a):
        if length != 4:
            moves = [from_place(a, d) for d in range(1, length)]
            return moves, lambda moves: [a, *moves]
        two = from_place(a, 2)
        after = on_line(a, [(i + 1, i) for i in range(3)])
        before = on_line(a, [(i, i + 1) for i in range(3)])

        def finish(moves):
            two, after, before = moves
            ends = on_line(two, [(2, 3), (1, 0)])
            after = jnp.where(line == 3, ends, after)
            return [a, after, two, jnp.where(line == 0, ends, before)]

        return [two, after, before], finish

    def sides(a):
        left, right = a[:, :local], a[:, local:]
        return jnp.where(first, left, right), jnp.where(first, right, left)

    def line_sum(hold, send):
        if length == 4:
            one, two, three = send
            relay = on_line(jnp.where(line == 0, three, one), [(0, 1), (3, 2)])
            after = on_line(one, [(i, i + 1) for i in range(3)])
            before = on_line(three, [(i + 1, i) for i in range(3)])
            mine, given = sides((two.astype(F32) + relay.astype(F32)).astype(BF16))
            mine = from_place(mine, 2)
            given = lax.ppermute(given, "an", [(i, (i + 4) % 8 ^ 1) for i in range(n)])
            keep, give = sides(hold + after.astype(F32) + before.astype(F32))
            got = swap_pair(give.astype(BF16))
            return keep + mine.astype(F32), got.astype(F32) + given.astype(F32)
        for i, a in enumerate(send):
            hold = hold + from_place(a, length - 1 - i).astype(F32)
        keep, give = sides(hold)
        return keep, swap_pair(give.astype(BF16))

    def swap_pieces(pieces, bit, axis):
        return jnp.concatenate([pieces, swap_sa(pieces, bit)], axis=axis)

    def in_order(pieces, axis):
        if (local // s_total) % head_dim == 0:
            return pieces
        came, size = [0], pieces.shape[axis] // s_total
        for bit in bits:
            came += [k ^ bit for k in came]
        return jnp.concatenate(
            [
                lax.slice_in_dim(pieces, came.index(k) * size, (came.index(k) + 1) * size, axis=axis)
                for k in range(s_total)
            ],
            axis=axis,
        )

    def own_piece(a, axis):
        size = a.shape[axis] // s_total
        return lax.dynamic_slice_in_dim(a, lax.axis_index("sa") * size, size, axis)

    low, high = decoder_states[:half], decoder_states[half:]
    mine = jnp.where(first, low, high)
    other = swap_pair(jnp.where(first, high, low))
    owner = requests // nb_own
    local_id = requests % nb_own
    owner_range = jnp.arange(n, dtype=jnp.int32)
    local_range = jnp.arange(nb_own, dtype=jnp.int32)
    hits = (owner[:, None, None] == owner_range[None, :, None]) & (
        local_id[:, None, None] == local_range[None, None, :]
    )
    present = jnp.max(hits.astype(jnp.int32), axis=0)
    earlier = (local_range[None, :] < local_range[:, None]).astype(jnp.int32)
    ranked = jnp.sum(present[:, None, :] * earlier[None, :, :], axis=2)
    rank_of_request = jnp.sum(jnp.where(hits, ranked[None], 0), axis=(1, 2))
    is_me = owner_range[:, None] == position
    my_present = jnp.sum(jnp.where(is_me, present, 0), axis=0)
    my_rank = jnp.sum(jnp.where(is_me, ranked, 0), axis=0)
    chosen_mask = (my_present[:, None] == 1) & (
        my_rank[:, None] == jnp.arange(per_owner, dtype=jnp.int32)[None, :]
    )
    local_of_slot = jnp.sum(jnp.where(chosen_mask, local_range[:, None], 0), axis=0)
    away = (owner // 2 - line + length) % length
    over = (owner % 2 != pair).astype(jnp.int32)
    where = (away * 2 + over) * per_owner + rank_of_request
    where = jnp.where(first, where[: total_requests // 2], where[total_requests // 2 :])

    tie = lax.optimization_barrier
    bits = [s_total >> k for k in range(1, s_total.bit_length())]
    rows_each = per_owner * span
    everything = jnp.zeros((n * rows_each, width), BF16)

    def put(everything, a, d, over):
        return lax.dynamic_update_slice_in_dim(everything, a, (d * 2 + over) * rows_each, 0)

    mine_near, mine_finish = line_gather(mine)
    encoded = encode(neighbour_inputs, local_of_slot, enc_up, enc_down)
    encoded, other, mine_near = tie((encoded, other, mine_near))

    packed = swap_pair(
        jnp.concatenate([own_piece(w, 1) for w in (w_query, w_key, w_value)], axis=0)
    )
    near, finish = line_gather(encoded)
    crossed = {0: swap_pair(encoded)}
    mine_line = mine_finish(mine_near)
    near, crossed[0], mine_line, packed, piece, encoded, other = tie(
        (near, crossed[0], mine_line, packed, own_piece(w_out, 0), encoded, other)
    )

    blocks = finish(near)
    crossed[length // 2] = swap_pair(blocks[length // 2])
    other_near, other_finish = line_gather(other)
    packed = swap_pieces(packed, bits[0], 1)
    piece = swap_pair(piece)
    blocks, crossed = tie((blocks, crossed))
    for d in range(length):
        everything = put(everything, blocks[d], d, 0)
    for d in crossed:
        everything = put(everything, crossed[d], d, 1)
    late = [swap_pair(blocks[d]) for d in range(length) if d not in crossed]
    other_near, piece, packed = tie((other_near, piece, packed))

    other_line = other_finish(other_near)
    for bit in bits[1:]:
        packed = swap_pieces(packed, bit, 1)
    for bit in bits:
        piece = swap_pieces(piece, bit, 0)
    packed, piece = in_order(packed, 1), in_order(piece, 0)
    late, everything = tie((late, everything))
    for d, a in zip([d for d in range(length) if d not in crossed], late):
        everything = put(everything, a, d, 1)
    everything = everything.reshape(n * per_owner, span, width)
    order = (line + jnp.arange(length, dtype=jnp.int32)) % length

    chunks = []
    split = 1
    rows, asked = half // split, where.shape[0] // split
    for k in range(split):
        queries = []
        for weight in (w_query, packed[:D]):
            total = 0.0
            for d in range(length):
                for x, y in ((mine_line[d], pair), (other_line[d], 1 - pair)):
                    part = lax.dynamic_slice_in_dim(
                        weight, (order[d] * 2 + y) * local, local, 0
                    )
                    total = total + jnp.dot(x, part, preferred_element_type=F32)
            queries.append(total.astype(BF16))
        queries = jnp.concatenate(queries, axis=1)
        attended = attend(
            where[k * asked : (k + 1) * asked],
            everything,
            queries,
            w_key,
            w_value,
            packed,
            head_dim,
            min(4, asked // NEIGH),
        )
        hold, *send = terms(order, attended, w_out, piece)
        chunks.append([a.astype(BF16) for a in line_sum(hold, send)])
    keep = jnp.concatenate([c[0] for c in chunks], axis=0)
    got = jnp.concatenate([c[1] for c in chunks], axis=0)
    return jnp.concatenate([jnp.where(first, keep, got), jnp.where(first, got, keep)], axis=0)


def solution(mesh):
    placed = (
        P("sa", "an"),
        P(None, "an"),
        P(None, "an"),
        P(None, "an"),
        P("an", None),
        P(),
        P(),
        P(("sa", "an"), None, None),
        P("sa"),
    )
    return jax.shard_map(
        shards, mesh=mesh, in_specs=placed, out_specs=P("sa", "an"), check_vma=False
    )
```
